32 devices in a mesh: dp: 4 (over z), row: 4 (over y, core), col: 2 (over x).
Axes of the slice: x: 2, y: 2, z: 4, core: 2. Of those that a mesh axis runs over, the one named last changes fastest.
Arguments:
- tokens: bfloat16 [768, 4096], P('row', ('dp', 'col')), may hold values from -6 to 6
- condition: bfloat16 [16, 768], P(('dp', 'row'), 'col'), may hold values from -6 to 6
- w_mod: bfloat16 [6, 768, 768], P(None, 'row', 'col'), may hold values from -0.21875 to 0.21875
- b_mod: bfloat16 [6, 768], P(None, 'row'), may hold values from -3 to 3
- w_query: bfloat16 [768, 768], P('row', 'col'), may hold values from -0.21875 to 0.21875
- w_key: bfloat16 [768, 768], P('row', 'col'), may hold values from -0.21875 to 0.21875
- w_value: bfloat16 [768, 768], P('row', 'col'), may hold values from -0.21875 to 0.21875
- b_query: bfloat16 [768], P('col'), may hold values from -3 to 3
- b_value: bfloat16 [768], P('col'), may hold values from -3 to 3
- w_out: bfloat16 [768, 768], P('row', 'col'), may hold values from -0.875 to 0.875
- b_out: bfloat16 [768], P('row'), may hold values from -2 to 2
- w_up: bfloat16 [768, 3072], P('row', 'col'), may hold values from -0.21875 to 0.21875
- b_up: bfloat16 [3072], P('col'), may hold values from -3 to 3
- w_down: bfloat16 [768, 3072], P('row', 'col'), may hold values from -0.109375 to 0.109375
- b_down: bfloat16 [768], P('row'), may hold values from -2 to 2
- cotangent: bfloat16 [768, 4096], P('row', ('dp', 'col')), may hold values from -6 to 6
Outputs:
- output: bfloat16 [768, 4096], P('row', ('dp', 'col'))
- grad_tokens: float32 [768, 4096], P('row', ('dp', 'col'))
- grad_condition: float32 [16, 768], P(('dp', 'row'), 'col')
- grad_w_mod: float32 [6, 768, 768], P(None, 'row', 'col')
- grad_b_mod: float32 [6, 768], P(None, 'row')
- grad_w_query: float32 [768, 768], P('row', 'col')
- grad_w_key: float32 [768, 768], P('row', 'col')
- grad_w_value: float32 [768, 768], P('row', 'col')
- grad_b_query: float32 [768], P('col')
- grad_b_value: float32 [768], P('col')
- grad_w_out: float32 [768, 768], P('row', 'col')
- grad_b_out: float32 [768], P('row')
- grad_w_up: float32 [768, 3072], P('row', 'col')
- grad_b_up: float32 [3072], P('col')
- grad_w_down: float32 [768, 3072], P('row', 'col')
- grad_b_down: float32 [768], P('row')
The draws below stay inside these ranges and needn't reach their ends.
All inputs are finite; a program needn't handle non-finite values.
Results may differ from the reference program's by a relative error of at most 0.02.
Values may be sent and summed in bfloat16 or wider, within the bound.
A program may use at most 128 MiB of HBM per device.

```python
import math
import jax
import jax.numpy as jnp
from jax import lax

D = 768
HEADS = 12
HEAD_DIM = 64
FF = 3072
LEN = 256
SEQS = 16
TOKENS = 4096


def steps_of(own_key, shape, shards, smallest, top_value):
    def one(dim, blocks):
        steps = jax.random.uniform(jax.random.fold_in(jax.random.fold_in(own_key, 6), dim), (blocks,), jnp.float32, smallest / len(shards), top_value / len(shards))
        return jnp.repeat(jnp.exp(steps), shape[dim] // blocks).reshape((-1,) + (1,) * (len(shape) - dim - 1))

    factor_of = one(*shards[0])
    for cut in shards[1:]:
        factor_of = factor_of * one(*cut)
    return factor_of


def gaussian(own_key, shape, scale, most, split=(), held_as=jnp.bfloat16):
    result = scale * jax.random.normal(own_key, shape, jnp.float32)
    if split:
        result = result * steps_of(own_key, shape, split, -0.22, 0.18)
    return jnp.clip(result, -most, most).astype(held_as)


def setup_inputs(seed: int = 0) -> dict:
    key_of = jax.random.split(jax.random.key(seed), 17)
    tokens = gaussian(key_of[0], (D, TOKENS), 1.0, 6.0, ((0, 4), (1, 8)))
    condition = gaussian(key_of[1], (SEQS, D), 1.0, 6.0, ((0, 16), (1, 2)))
    w_mod = gaussian(key_of[2], (6, D, D), D ** -0.5, 0.21875, ((1, 4), (2, 2)))
    b_mod = gaussian(key_of[3], (6, D), 0.5, 3.0, ((1, 4),))
    w_query = gaussian(key_of[4], (D, D), D ** -0.5, 0.21875, ((0, 4), (1, 2)))
    w_key = gaussian(key_of[5], (D, D), D ** -0.5, 0.21875, ((0, 4), (1, 2)))
    w_value = gaussian(key_of[6], (D, D), D ** -0.5, 0.21875, ((0, 4), (1, 2)))
    b_query = gaussian(key_of[7], (D,), 0.5, 3.0, ((0, 2),))
    b_value = gaussian(key_of[8], (D,), 0.5, 3.0, ((0, 2),))
    w_out = gaussian(key_of[9], (D, D), (D // 16) ** -0.5, 0.875, ((0, 4), (1, 2)))
    b_out = gaussian(key_of[10], (D,), 0.3, 2.0, ((0, 4),))
    w_up = gaussian(key_of[11], (D, FF), D ** -0.5, 0.21875, ((0, 4), (1, 2)))
    b_up = gaussian(key_of[12], (FF,), 0.5, 3.0, ((0, 2),))
    w_down = gaussian(key_of[13], (D, FF), FF ** -0.5, 0.109375, ((0, 4), (1, 2)))
    b_down = gaussian(key_of[14], (D,), 0.3, 2.0, ((0, 4),))
    cotangent = gaussian(key_of[15], (D, TOKENS), 1.0, 6.0, ((0, 4), (1, 8)))
    return dict(tokens=tokens, condition=condition, w_mod=w_mod, b_mod=b_mod, w_query=w_query, w_key=w_key, w_value=w_value, b_query=b_query, b_value=b_value, w_out=w_out, b_out=b_out, w_up=w_up, b_up=b_up, w_down=w_down, b_down=b_down, cotangent=cotangent)


@jax.custom_vjp
def low(v):
    return lax.optimization_barrier(v.astype(jnp.bfloat16)).astype(jnp.float32)

@jax.custom_vjp
def low_back(v):
    return v

def low_keep(v):
    return (low(v), None)

def low_pass(kept, grad):
    return (grad,)

def back_keep(v):
    return (v, None)

def back_low(kept, grad):
    return (low(grad),)
low.defvjp(low_keep, low_pass)
low_back.defvjp(back_keep, back_low)
HIGHEST_PRECISION = lax.Precision.HIGHEST

def rounded(values):
    return low_back(low(values))

def matmul(left_side, right_side):
    return jnp.dot(left_side, right_side, precision=HIGHEST_PRECISION)

def layer_norm(values):
    centre = values - lax.optimization_barrier(jnp.mean(values, axis=-1, keepdims=True))
    spread = lax.optimization_barrier(jnp.mean(centre * centre, axis=-1, keepdims=True))
    return centre * lax.rsqrt(spread + 1e-06)

def attend(query_block, key_block, value_block):
    scores = jnp.einsum('bqhe,bkhe->bhqk', query_block, key_block, precision=HIGHEST_PRECISION) * HEAD_DIM ** (-0.5)
    scores = low_back(scores)
    weights = low(jax.nn.softmax(scores, axis=-1))
    return jnp.einsum('bhqk,bkhe->bqhe', weights, value_block, precision=HIGHEST_PRECISION)

def attend_block(triple):
    return jax.checkpoint(attend)(triple[0], triple[1], triple[2])

def forward(tokens, condition, w_mod, b_mod, w_query, w_key, w_value, b_query, b_value, w_out, b_out, w_up, b_up, w_down, b_down):
    latents = condition.shape[0]
    silu_cond = low(jax.nn.silu(condition))
    modulation = low_back(jnp.einsum('sd,ked->ske', silu_cond, w_mod, precision=HIGHEST_PRECISION) + b_mod)
    shift_attn = modulation[:, 0][:, None, :]
    scale_attn = modulation[:, 1][:, None, :]
    gate_attn = modulation[:, 2][:, None, :]
    shift_mlp = modulation[:, 3][:, None, :]
    scale_mlp = modulation[:, 4][:, None, :]
    gate_mlp = modulation[:, 5][:, None, :]
    residual = tokens.T.reshape(latents, LEN, D)
    normed = layer_norm(residual) * (1.0 + scale_attn) + shift_attn
    hidden_attn = low(normed.reshape(-1, D))
    queries = rounded(matmul(hidden_attn, w_query) + b_query)
    keys_all = rounded(matmul(hidden_attn, w_key))
    values_all = rounded(matmul(hidden_attn, w_value) + b_value)
    group_size = math.gcd(latents, 16)

    def split_heads(matrix):
        return matrix.reshape(latents // group_size, group_size, LEN, HEADS, HEAD_DIM)
    mixture = lax.map(attend_block, (split_heads(queries), split_heads(keys_all), split_heads(values_all)))
    attended = rounded(mixture.reshape(-1, D))
    projected = low_back(matmul(attended, w_out.T) + b_out)
    residual = residual + gate_attn * projected.reshape(latents, LEN, D)
    normed = layer_norm(residual) * (1.0 + scale_mlp) + shift_mlp
    hidden_mlp = low(normed.reshape(-1, D))
    upward = low_back(matmul(hidden_mlp, w_up) + b_up)
    activated = low(jax.nn.gelu(upward, approximate=True))
    downward = low_back(matmul(activated, w_down.T) + b_down)
    residual = residual + gate_mlp * downward.reshape(latents, LEN, D)
    return residual.reshape(-1, D).T

def reference(tokens, condition, w_mod, b_mod, w_query, w_key, w_value, b_query, b_value, w_out, b_out, w_up, b_up, w_down, b_down, cotangent):
    inputs = tuple((argument.astype(jnp.float32) for argument in (tokens, condition, w_mod, b_mod, w_query, w_key, w_value, b_query, b_value, w_out, b_out, w_up, b_up, w_down, b_down)))
    output, pullback = jax.vjp(forward, *inputs)
    gradients = pullback(cotangent.astype(jnp.float32))
    return (output.astype(jnp.bfloat16), gradients[0], gradients[1], gradients[2], gradients[3], gradients[4], gradients[5], gradients[6], gradients[7], gradients[8], gradients[9], gradients[10], gradients[11], gradients[12], gradients[13], gradients[14])
```

```python
from functools import partial

import jax
import jax.numpy as jnp
from jax import lax
from jax.sharding import PartitionSpec as P

D = 768
HEAD_DIM = 64
LEN = 256
ORDER = (0, 2, 1, 3)
F32 = jnp.float32
BF16 = jnp.bfloat16


def contract(left, right, left_dim, right_dim):
    return lax.dot_general(
        left, right, (((left_dim,), (right_dim,)), ((), ())), preferred_element_type=F32
    )


def contract_heads(left, right, left_dim, right_dim):
    return lax.dot_general(
        left, right, (((left_dim,), (right_dim,)), ((0,), (0,))), preferred_element_type=F32
    )


def swap_row(value, offset):
    size = lax.axis_size("row")
    return lax.ppermute(value, "row", [(i, i ^ offset) for i in range(size)])


def swap_col(value):
    return lax.ppermute(value, "col", [(0, 1), (1, 0)])


def after(value, earlier):
    return lax.optimization_barrier((value, earlier))[0]


def gather_row(shard, far=None):
    if far is None:
        far = swap_row(shard, 2)
    return jnp.concatenate([shard, far, swap_row(shard, 1), swap_row(far, 1)], axis=0)


def pair_sum(partial_sum):
    mine = partial_sum.astype(BF16)
    return mine.astype(F32) + swap_col(mine).astype(F32)


def scatter_row(full):
    half = full.shape[0] // 2
    quarter = half // 2
    near = full[:half].astype(F32) + swap_row(full[half:], 1).astype(F32)
    near = near.astype(BF16)
    own = near[:quarter].astype(F32) + swap_row(near[quarter:], 2).astype(F32)
    return own.astype(BF16)


def sum_dp(value):
    size = lax.axis_size("dp")
    place = lax.axis_index("dp") % 4
    inner = jnp.logical_or(place == 1, place == 2)
    inward = [(i, i + 1) if i % 4 == 0 else (i, i - 1) for i in range(size) if i % 4 in (0, 3)]
    middle = [(i, i ^ 3) for i in range(size) if i % 4 in (1, 2)]
    outward = [(b, a) for a, b in inward]
    first = (value.astype(F32) + lax.ppermute(value, "dp", inward).astype(F32)).astype(BF16)
    total = first.astype(F32) + lax.ppermute(first, "dp", middle).astype(F32)
    total = total.astype(BF16)
    step = 4
    while step < size:
        other = lax.ppermute(total, "dp", [(i, i ^ step) for i in range(size)])
        total = (total.astype(F32) + other.astype(F32)).astype(BF16)
        step *= 2
    back = lax.ppermute(total, "dp", outward)
    return jnp.where(inner, total, back).astype(F32)


def latent_of(local, row, col):
    per_col = local.shape[1] // LEN
    both = jnp.concatenate([local, swap_col(local)], axis=1)

    def block(latent):
        place = jnp.where(latent // per_col == col, 0, per_col) + latent % per_col
        return lax.dynamic_slice_in_dim(both, place * LEN, LEN, axis=1)

    return jnp.concatenate(
        [block(row)] + [swap_row(block(row ^ k), k) for k in ORDER[1:]], axis=0
    )


def spread_out(full, row, col):
    rows, cols = lax.axis_size("row"), lax.axis_size("col")
    per_col = rows // cols
    width = full.shape[0] // rows
    got = {0: full[:width]}
    for place, k in enumerate(ORDER):
        if k:
            pairs = [(r * cols + r // per_col, (r ^ k) * cols + r // per_col) for r in range(rows)]
            got[k] = lax.ppermute(
                full[place * width : (place + 1) * width], ("row", "col"), pairs
            )
    here = row // per_col == col
    first = jnp.where(here, got[0], got[2])
    second = jnp.where(here, got[1], got[3])
    even = row % 2 == 0
    return jnp.concatenate(
        [jnp.where(even, first, second), jnp.where(even, second, first)], axis=1
    )


def normalize(values):
    centre = jnp.mean(values, axis=0, keepdims=True)
    moved = values - centre
    inverse = lax.rsqrt(jnp.mean(moved * moved, axis=0, keepdims=True) + 1e-06)
    return moved * inverse, inverse


def normalize_back(grad, normed, inverse):
    return inverse * (
        grad
        - jnp.mean(grad, axis=0, keepdims=True)
        - normed * jnp.mean(grad * normed, axis=0, keepdims=True)
    )


def body(
    tokens,
    condition,
    w_mod,
    b_mod,
    w_query,
    w_key,
    w_value,
    b_query,
    b_value,
    w_out,
    b_out,
    w_up,
    b_up,
    w_down,
    b_down,
    cotangent,
):
    row = lax.axis_index("row")
    col = lax.axis_index("col")
    rows = lax.axis_size("row")
    width_row = tokens.shape[0]
    width_col = w_query.shape[1]
    heads = width_col // HEAD_DIM

    w_joined_own = jnp.concatenate([w_query, w_key, w_value], axis=1)
    far_joined = swap_row(w_joined_own, 2)
    far_out = swap_row(after(w_out, far_joined), 2)
    far_up = swap_row(after(w_up, far_out), 2)
    far_down = swap_row(after(w_down, far_up), 2)
    w_joined = gather_row(w_joined_own, far_joined)
    w_out_all = gather_row(w_out, far_out)
    w_up_all = gather_row(w_up, far_up)
    w_down_all = gather_row(w_down, far_down)

    condition_float = condition.astype(F32)
    silu_cond = jax.nn.silu(condition_float).astype(BF16)
    cond_rows = jnp.concatenate(
        [silu_cond] + [swap_row(silu_cond, k) for k in ORDER[1:]], axis=0
    )
    mod_flat = w_mod.reshape(-1, w_mod.shape[2])
    terms = contract(cond_rows, mod_flat, 1, 1)
    terms = terms + swap_col(terms)
    terms = terms.reshape(rows, 6, width_row) + b_mod.astype(F32)[None]
    extra = jnp.stack([b_out, b_down]).astype(F32)
    packed = jnp.concatenate([terms, jnp.broadcast_to(extra[None], (rows, 2, width_row))], axis=1)
    vectors = jnp.concatenate(
        [packed[0]] + [swap_row(packed[i], k) for i, k in enumerate(ORDER) if k], axis=1
    )
    columns = vectors.T
    shift_attn, scale_attn, gate_attn, shift_mlp, scale_mlp, gate_mlp, bias_out, bias_down = (
        columns[:, i : i + 1] for i in range(8)
    )

    x = latent_of(tokens, row, col).astype(F32)
    normed_attn, inverse_attn = normalize(x)
    hidden_attn = (normed_attn * (1.0 + scale_attn) + shift_attn).astype(BF16)
    joined = contract(w_joined, hidden_attn, 0, 0)

    def split_heads(matrix):
        return matrix.reshape(heads, HEAD_DIM, LEN)

    queries = split_heads((joined[:width_col] + b_query.astype(F32)[:, None]).astype(BF16))
    keys = split_heads(joined[width_col : 2 * width_col].astype(BF16))
    values = split_heads((joined[2 * width_col :] + b_value.astype(F32)[:, None]).astype(BF16))
    scale_factor = HEAD_DIM ** (-0.5)
    scores = contract_heads(queries, keys, 1, 1) * scale_factor
    exponent = jnp.exp(scores - jnp.max(scores, axis=-1, keepdims=True))
    full_probs = exponent / jnp.sum(exponent, axis=-1, keepdims=True)
    probabilities = full_probs.astype(BF16)
    attended = contract_heads(values, probabilities, 2, 2).reshape(width_col, LEN).astype(BF16)
    projected = pair_sum(contract(w_out_all, attended, 1, 0)) + bias_out
    residual = x + gate_attn * projected

    normed_mlp, inverse_mlp = normalize(residual)
    hidden_mlp = (normed_mlp * (1.0 + scale_mlp) + shift_mlp).astype(BF16)
    upward = contract(w_up_all, hidden_mlp, 0, 0) + b_up.astype(F32)[:, None]
    activated, gelu_back = jax.vjp(partial(jax.nn.gelu, approximate=True), upward)
    activated = activated.astype(BF16)
    downward = pair_sum(contract(w_down_all, activated, 1, 0)) + bias_down
    output = spread_out((residual + gate_mlp * downward).astype(BF16), row, col)

    cot = latent_of(cotangent, row, col).astype(F32)
    grad_gate_mlp = jnp.sum(cot * downward, axis=1)
    grad_down = (cot * gate_mlp).astype(BF16)
    grad_activated = contract(w_down_all, grad_down, 0, 0)
    grad_w_down = sum_dp(scatter_row(contract(grad_down, activated, 1, 1).astype(BF16)))
    grad_b_down = jnp.sum(grad_down.astype(F32), axis=1)
    grad_upward = gelu_back(grad_activated)[0].astype(BF16)
    grad_hidden = pair_sum(contract(w_up_all, grad_upward, 1, 0))
    grad_w_up = sum_dp(scatter_row(contract(hidden_mlp, grad_upward, 1, 1).astype(BF16)))
    grad_b_up = jnp.sum(grad_upward.astype(F32), axis=1)
    grad_scale_mlp = jnp.sum(grad_hidden * normed_mlp, axis=1)
    grad_shift_mlp = jnp.sum(grad_hidden, axis=1)
    grad_residual = cot + normalize_back(grad_hidden * (1.0 + scale_mlp), normed_mlp, inverse_mlp)

    grad_gate_attn = jnp.sum(grad_residual * projected, axis=1)
    grad_projected = (grad_residual * gate_attn).astype(BF16)
    grad_w_out = sum_dp(scatter_row(contract(grad_projected, attended, 1, 1).astype(BF16)))
    grad_b_out = jnp.sum(grad_projected.astype(F32), axis=1)
    grad_heads = split_heads(contract(w_out_all, grad_projected, 0, 0).astype(BF16))
    grad_probs = contract_heads(grad_heads, values, 1, 1)
    grad_values = contract_heads(grad_heads, probabilities, 2, 1)
    inner = jnp.sum(full_probs * grad_probs, axis=-1, keepdims=True)
    grad_scores = (full_probs * (grad_probs - inner)).astype(BF16)
    grad_queries = contract_heads(keys, grad_scores, 2, 2) * scale_factor
    grad_keys = contract_heads(queries, grad_scores, 2, 1) * scale_factor
    grad_joined = jnp.concatenate(
        [part.reshape(width_col, LEN).astype(BF16) for part in (grad_queries, grad_keys, grad_values)],
        axis=0,
    )
    grad_hidden = pair_sum(contract(w_joined, grad_joined, 1, 0))
    grad_w_joined = sum_dp(scatter_row(contract(hidden_attn, grad_joined, 1, 1).astype(BF16)))
    grad_b_joined = jnp.sum(grad_joined.astype(F32), axis=1)
    grad_scale_attn = jnp.sum(grad_hidden * normed_attn, axis=1)
    grad_shift_attn = jnp.sum(grad_hidden, axis=1)
    grad_x = grad_residual + normalize_back(
        grad_hidden * (1.0 + scale_attn), normed_attn, inverse_attn
    )
    grad_tokens = spread_out(grad_x.astype(BF16), row, col).astype(F32)

    own_vectors = jnp.stack(
        [
            grad_shift_attn,
            grad_scale_attn,
            grad_gate_attn,
            grad_shift_mlp,
            grad_scale_mlp,
            grad_gate_mlp,
            grad_b_down,
            grad_b_out,
        ]
    ).astype(BF16)
    pieces = [own_vectors[:, i * width_row : (i + 1) * width_row] for i in range(rows)]
    by_latent = jnp.stack([pieces[0]] + [swap_row(pieces[i], k) for i, k in enumerate(ORDER) if k])
    grad_mod = by_latent[:, :6].reshape(rows, -1)
    grad_silu = contract(grad_mod, mod_flat, 1, 0)
    grad_silu = grad_silu[0:1] + sum(
        swap_row(grad_silu[i : i + 1], k) for i, k in enumerate(ORDER) if k
    )
    grad_condition = jax.vjp(jax.nn.silu, condition_float)[1](grad_silu)[0]
    message = jnp.concatenate([by_latent.reshape(rows, -1), cond_rows], axis=1)
    everyone = lax.all_gather(message, "dp", axis=0, tiled=True)
    all_mod = everyone[:, : 6 * width_row]
    all_cond = everyone[:, 8 * width_row :]
    grad_w_mod = contract(all_mod, all_cond, 0, 0).reshape(w_mod.shape)
    sums = jnp.sum(everyone[:, : 8 * width_row].astype(F32), axis=0)
    grad_b_mod = sums[: 6 * width_row].reshape(b_mod.shape)
    grad_b_down = sums[6 * width_row : 7 * width_row]
    grad_b_out = sums[7 * width_row :]
    bias_sums = lax.psum(
        jnp.concatenate([grad_b_up, grad_b_joined[:width_col], grad_b_joined[2 * width_col :]]),
        ("dp", "row"),
    )
    hidden_width = grad_b_up.shape[0]
    return (
        output,
        grad_tokens,
        grad_condition,
        grad_w_mod,
        grad_b_mod,
        grad_w_joined[:, :width_col],
        grad_w_joined[:, width_col : 2 * width_col],
        grad_w_joined[:, 2 * width_col :],
        bias_sums[hidden_width : hidden_width + width_col],
        bias_sums[hidden_width + width_col :],
        grad_w_out,
        grad_b_out,
        grad_w_up,
        bias_sums[:hidden_width],
        grad_w_down,
        grad_b_down,
    )


def solution(mesh):
    placed = (
        P("row", ("dp", "col")),
        P(("dp", "row"), "col"),
        P(None, "row", "col"),
        P(None, "row"),
        P("row", "col"),
        P("row", "col"),
        P("row", "col"),
        P("col"),
        P("col"),
        P("row", "col"),
        P("row"),
        P("row", "col"),
        P("col"),
        P("row", "col"),
        P("row"),
        P("row", ("dp", "col")),
    )
    return jax.shard_map(
        body,
        mesh=mesh,
        in_specs=placed,
        out_specs=(
            P("row", ("dp", "col")),
            P("row", ("dp", "col")),
            P(("dp", "row"), "col"),
            P(None, "row", "col"),
            P(None, "row"),
            P("row", "col"),
            P("row", "col"),
            P("row", "col"),
            P("col"),
            P("col"),
            P("row", "col"),
            P("row"),
            P("row", "col"),
            P("col"),
            P("row", "col"),
            P("row"),
        ),
        check_vma=False,
    )
```

```python
from functools import partial

import jax
import jax.numpy as jnp
from jax import lax
from jax.sharding import PartitionSpec as P

D = 768
HEAD_DIM = 64
LEN = 256
ORDER = (0, 2, 1, 3)
F32 = jnp.float32
BF16 = jnp.bfloat16


def contract(left, right, left_dim, right_dim):
    return lax.dot_general(
        left, right, (((left_dim,), (right_dim,)), ((), ())), preferred_element_type=F32
    )


def contract_heads(left, right, left_dim, right_dim):
    return lax.dot_general(
        left, right, (((left_dim,), (right_dim,)), ((0,), (0,))), preferred_element_type=F32
    )


def swap_row(value, offset):
    size = lax.axis_size("row")
    return lax.ppermute(value, "row", [(i, i ^ offset) for i in range(size)])


def swap_col(value):
    return lax.ppermute(value, "col", [(0, 1), (1, 0)])


def after(value, earlier):
    return lax.optimization_barrier((value, earlier))[0]


def gather_row(shard, far=None):
    if far is None:
        far = swap_row(shard, 2)
    return jnp.concatenate([shard, far, swap_row(shard, 1), swap_row(far, 1)], axis=0)


def pair_sum(partial_sum):
    mine = partial_sum.astype(BF16)
    return mine.astype(F32) + swap_col(mine).astype(F32)


def near_sum(left, right):
    half = left.shape[0] // 2
    quarter = half // 2
    other = swap_row(contract(left[half:], right, 1, 1).astype(BF16), 1)
    own = contract(left[:quarter], right, 1, 1) + other[:quarter].astype(F32)
    far = contract(left[quarter:half], right, 1, 1) + other[quarter:].astype(F32)
    return own, far.astype(BF16)


def far_sum(near):
    return (near[0] + swap_row(near[1], 2).astype(F32)).astype(BF16)


def dp_pairs():
    size = lax.axis_size("dp")
    inward = [(i, i + 1) if i % 4 == 0 else (i, i - 1) for i in range(size) if i % 4 in (0, 3)]
    middle = [(i, i ^ 3) for i in range(size) if i % 4 in (1, 2)]
    return inward, middle, [(b, a) for a, b in inward]


def dp_first(value):
    return (value.astype(F32) + lax.ppermute(value, "dp", dp_pairs()[0]).astype(F32)).astype(BF16)


def dp_second(first):
    size = lax.axis_size("dp")
    total = first.astype(F32) + lax.ppermute(first, "dp", dp_pairs()[1]).astype(F32)
    total = total.astype(BF16)
    step = 4
    while step < size:
        other = lax.ppermute(total, "dp", [(i, i ^ step) for i in range(size)])
        total = (total.astype(F32) + other.astype(F32)).astype(BF16)
        step *= 2
    return total


def dp_third(total):
    place = lax.axis_index("dp") % 4
    inner = jnp.logical_or(place == 1, place == 2)
    back = lax.ppermute(total, "dp", dp_pairs()[2])
    return jnp.where(inner, total, back).astype(F32)


def gather_dp(value):
    size = lax.axis_size("dp")
    place = lax.axis_index("dp")
    step = 1
    while step < size:
        other = lax.ppermute(value, "dp", [(i, i ^ step) for i in range(size)])
        upper = (place // step) % 2 == 1
        value = jnp.concatenate(
            [jnp.where(upper, other, value), jnp.where(upper, value, other)], axis=0
        )
        step *= 2
    return value


def beside(columns):
    lane = lax.broadcasted_iota(jnp.int32, (1, len(columns)), 1)
    return sum(jnp.where(lane == i, column, 0.0) for i, column in enumerate(columns))


def latent_of(local, row, col):
    per_col = local.shape[1] // LEN
    both = jnp.concatenate([local, swap_col(local)], axis=1)

    def block(latent):
        place = jnp.where(latent // per_col == col, 0, per_col) + latent % per_col
        return lax.dynamic_slice_in_dim(both, place * LEN, LEN, axis=1)

    return jnp.concatenate(
        [block(row)] + [swap_row(block(row ^ k), k) for k in ORDER[1:]], axis=0
    )


def spread_out(full, row, col):
    rows, cols = lax.axis_size("row"), lax.axis_size("col")
    per_col = rows // cols
    width = full.shape[0] // rows
    got = {0: full[:width]}
    for place, k in enumerate(ORDER):
        if k:
            pairs = [(r * cols + r // per_col, (r ^ k) * cols + r // per_col) for r in range(rows)]
            got[k] = lax.ppermute(
                full[place * width : (place + 1) * width], ("row", "col"), pairs
            )
    here = row // per_col == col
    first = jnp.where(here, got[0], got[2])
    second = jnp.where(here, got[1], got[3])
    even = row % 2 == 0
    return jnp.concatenate(
        [jnp.where(even, first, second), jnp.where(even, second, first)], axis=1
    )


def normalize(values):
    centre = jnp.mean(values, axis=0, keepdims=True)
    moved = values - centre
    inverse = lax.rsqrt(jnp.mean(moved * moved, axis=0, keepdims=True) + 1e-06)
    return moved * inverse, inverse


def normalize_back(grad, normed, inverse):
    return inverse * (
        grad
        - jnp.mean(grad, axis=0, keepdims=True)
        - normed * jnp.mean(grad * normed, axis=0, keepdims=True)
    )


def body(
    tokens,
    condition,
    w_mod,
    b_mod,
    w_query,
    w_key,
    w_value,
    b_query,
    b_value,
    w_out,
    b_out,
    w_up,
    b_up,
    w_down,
    b_down,
    cotangent,
):
    row = lax.axis_index("row")
    col = lax.axis_index("col")
    rows = lax.axis_size("row")
    width_row = tokens.shape[0]
    width_col = w_query.shape[1]
    heads = width_col // HEAD_DIM

    w_joined_own = jnp.concatenate([w_query, w_key, w_value], axis=1)
    far_joined = swap_row(w_joined_own, 2)

    condition_float = condition.astype(F32)
    silu_cond = jax.nn.silu(condition_float).astype(BF16)
    cond_rows = jnp.concatenate(
        [silu_cond] + [swap_row(silu_cond, k) for k in ORDER[1:]], axis=0
    )
    mod_flat = w_mod.reshape(-1, w_mod.shape[2])
    terms = contract(cond_rows, mod_flat, 1, 1)
    terms = terms + swap_col(terms)
    terms = terms.reshape(rows, 6, width_row) + b_mod.astype(F32)[None]
    extra = jnp.stack([b_out, b_down]).astype(F32)
    packed = jnp.concatenate([terms, jnp.broadcast_to(extra[None], (rows, 2, width_row))], axis=1)
    vectors = jnp.concatenate(
        [packed[0]] + [swap_row(packed[i], k) for i, k in enumerate(ORDER) if k], axis=1
    )
    columns = vectors.T
    local_tokens = latent_of(tokens, row, col)
    held = (vectors, local_tokens, far_joined)
    far_out = swap_row(after(w_out, held), 2)
    far_up = swap_row(after(w_up, far_out), 2)
    far_down = swap_row(after(w_down, far_up), 2)
    cot = latent_of(after(cotangent, far_up), row, col).astype(F32)
    w_joined = gather_row(w_joined_own, far_joined)
    w_out_all = gather_row(w_out, far_out)
    w_up_all = gather_row(w_up, far_up)
    w_down_all = gather_row(w_down, far_down)
    shift_attn, scale_attn, gate_attn, shift_mlp, scale_mlp, gate_mlp, bias_out, bias_down = (
        columns[:, i : i + 1] for i in range(8)
    )

    x = local_tokens.astype(F32)
    normed_attn, inverse_attn = normalize(x)
    hidden_attn = (normed_attn * (1.0 + scale_attn) + shift_attn).astype(BF16)
    joined = contract(w_joined, hidden_attn, 0, 0)

    def split_heads(matrix):
        return matrix.reshape(heads, HEAD_DIM, LEN)

    queries = split_heads((joined[:width_col] + b_query.astype(F32)[:, None]).astype(BF16))
    keys = split_heads(joined[width_col : 2 * width_col].astype(BF16))
    values = split_heads((joined[2 * width_col :] + b_value.astype(F32)[:, None]).astype(BF16))
    scale_factor = HEAD_DIM ** (-0.5)
    scores = contract_heads(queries, keys, 1, 1) * scale_factor
    exponent = jnp.exp(scores - jnp.max(scores, axis=-1, keepdims=True))
    full_probs = exponent / jnp.sum(exponent, axis=-1, keepdims=True)
    probabilities = full_probs.astype(BF16)
    attended = contract_heads(values, probabilities, 2, 2).reshape(width_col, LEN).astype(BF16)
    projected = pair_sum(contract(w_out_all, attended, 1, 0)) + bias_out
    residual = x + gate_attn * projected

    normed_mlp, inverse_mlp = normalize(residual)
    hidden_mlp = (normed_mlp * (1.0 + scale_mlp) + shift_mlp).astype(BF16)
    upward = contract(w_up_all, hidden_mlp, 0, 0) + b_up.astype(F32)[:, None]
    activated, gelu_back = jax.vjp(partial(jax.nn.gelu, approximate=True), upward)
    activated = activated.astype(BF16)

    grad_down = (cot * gate_mlp).astype(BF16)
    grad_activated = contract(w_down_all, grad_down, 0, 0)
    grad_b_down = jnp.sum(grad_down.astype(F32), axis=1, keepdims=True)
    grad_upward = gelu_back(grad_activated)[0].astype(BF16)
    near_down = near_sum(grad_down, activated)
    grad_hidden = pair_sum(contract(w_up_all, grad_upward, 1, 0))
    near_up = near_sum(hidden_mlp, grad_upward)
    grad_b_up = jnp.sum(grad_upward.astype(F32), axis=1, keepdims=True)
    grad_hidden, near_down, near_up = lax.optimization_barrier((grad_hidden, near_down, near_up))
    sum_down = far_sum(near_down)
    grad_scale_mlp = jnp.sum(grad_hidden * normed_mlp, axis=1, keepdims=True)
    grad_shift_mlp = jnp.sum(grad_hidden, axis=1, keepdims=True)
    grad_residual = cot + normalize_back(grad_hidden * (1.0 + scale_mlp), normed_mlp, inverse_mlp)

    down_partial = after(contract(w_down_all, activated, 1, 0), grad_hidden)
    downward = pair_sum(down_partial) + bias_down
    output = spread_out((residual + gate_mlp * downward).astype(BF16), row, col)
    grad_gate_mlp = jnp.sum(cot * downward, axis=1, keepdims=True)

    grad_gate_attn = jnp.sum(grad_residual * projected, axis=1, keepdims=True)
    grad_projected = (grad_residual * gate_attn).astype(BF16)
    near_out = near_sum(grad_projected, attended)
    grad_b_out = jnp.sum(grad_projected.astype(F32), axis=1, keepdims=True)
    grad_heads = split_heads(contract(w_out_all, grad_projected, 0, 0).astype(BF16))
    grad_probs = contract_heads(grad_heads, values, 1, 1)
    grad_values = contract_heads(grad_heads, probabilities, 2, 1)
    grad_probs, sum_down = lax.optimization_barrier((grad_probs, sum_down))
    first_down = dp_first(sum_down)
    sum_up = far_sum(near_up)
    inner = jnp.sum(full_probs * grad_probs, axis=-1, keepdims=True)
    grad_scores = (full_probs * (grad_probs - inner)).astype(BF16)
    grad_queries = contract_heads(keys, grad_scores, 2, 2) * scale_factor
    grad_keys = contract_heads(queries, grad_scores, 2, 1) * scale_factor
    grad_joined = jnp.concatenate(
        [part.reshape(width_col, LEN).astype(BF16) for part in (grad_queries, grad_keys, grad_values)],
        axis=0,
    )
    grad_hidden = pair_sum(contract(w_joined, grad_joined, 1, 0))
    near_joined = near_sum(hidden_attn, grad_joined)
    grad_b_joined = jnp.sum(grad_joined.astype(F32), axis=1, keepdims=True)
    sum_out = far_sum(near_out)
    grad_hidden, near_joined, first_down, sum_up, sum_out, output = lax.optimization_barrier(
        (grad_hidden, near_joined, first_down, sum_up, sum_out, output)
    )
    total_down = dp_second(first_down)
    first_up = dp_first(sum_up)
    sum_joined = far_sum(near_joined)
    grad_scale_attn = jnp.sum(grad_hidden * normed_attn, axis=1, keepdims=True)
    grad_shift_attn = jnp.sum(grad_hidden, axis=1, keepdims=True)
    grad_x = grad_residual + normalize_back(
        grad_hidden * (1.0 + scale_attn), normed_attn, inverse_attn
    )
    grad_tokens = spread_out(grad_x.astype(BF16), row, col)

    own_vectors = beside(
        [
            grad_shift_attn,
            grad_scale_attn,
            grad_gate_attn,
            grad_shift_mlp,
            grad_scale_mlp,
            grad_gate_mlp,
            grad_b_down,
            grad_b_out,
        ]
    ).astype(BF16).T
    bias_grads = jnp.concatenate(
        [grad_b_up, grad_b_joined[:width_col], grad_b_joined[2 * width_col :]]
    ).reshape(-1, width_row).astype(BF16)
    pieces = [
        jnp.concatenate([own_vectors[:, i * width_row : (i + 1) * width_row], bias_grads])
        for i in range(rows)
    ]
    by_latent = jnp.stack([pieces[0]] + [swap_row(pieces[i], k) for i, k in enumerate(ORDER) if k])
    grad_mod = by_latent[:, :6].reshape(rows, -1)
    grad_silu = contract(grad_mod, mod_flat, 1, 0)
    grad_silu = grad_silu[0:1] + sum(
        swap_row(grad_silu[i : i + 1], k) for i, k in enumerate(ORDER) if k
    )
    grad_condition = jax.vjp(jax.nn.silu, condition_float)[1](grad_silu)[0]
    bias_terms = by_latent[:, 8:].astype(F32)
    bias_terms = (bias_terms[0] + bias_terms[1]) + (bias_terms[2] + bias_terms[3])
    message = jnp.concatenate(
        [
            by_latent[:, :8].reshape(rows, -1),
            cond_rows,
            bias_terms.astype(BF16).reshape(rows, -1),
        ],
        axis=1,
    )
    everyone = gather_dp(message)
    all_mod = everyone[:, : 6 * width_row]
    all_cond = everyone[:, 8 * width_row : 8 * width_row + width_col]
    grad_w_mod = contract(all_mod, all_cond, 0, 0).reshape(w_mod.shape)
    sums = jnp.sum(everyone[:, : 8 * width_row].astype(F32), axis=0)
    grad_b_mod = sums[: 6 * width_row].reshape(b_mod.shape)
    grad_b_down = sums[6 * width_row : 7 * width_row]
    grad_b_out = sums[7 * width_row :]
    bias_parts = everyone[:, 8 * width_row + width_col :].astype(F32)
    bias_sums = jnp.sum(bias_parts.reshape(-1, rows, bias_parts.shape[1]), axis=0).reshape(-1)
    hidden_width = grad_b_up.shape[0]

    first_out = dp_first(sum_out)
    first_joined = dp_first(sum_joined)
    total_up = dp_second(first_up)
    total_out = dp_second(first_out)
    total_joined = dp_second(first_joined)
    grad_w_down = dp_third(total_down)
    grad_w_up = dp_third(total_up)
    grad_w_out = dp_third(total_out)
    grad_w_joined = dp_third(total_joined)
    return (
        output,
        grad_tokens.astype(F32),
        grad_condition,
        grad_w_mod,
        grad_b_mod,
        grad_w_joined[:, :width_col],
        grad_w_joined[:, width_col : 2 * width_col],
        grad_w_joined[:, 2 * width_col :],
        bias_sums[hidden_width : hidden_width + width_col],
        bias_sums[hidden_width + width_col :],
        grad_w_out,
        grad_b_out,
        grad_w_up,
        bias_sums[:hidden_width],
        grad_w_down,
        grad_b_down,
    )


def solution(mesh):
    placed = (
        P("row", ("dp", "col")),
        P(("dp", "row"), "col"),
        P(None, "row", "col"),
        P(None, "row"),
        P("row", "col"),
        P("row", "col"),
        P("row", "col"),
        P("col"),
        P("col"),
        P("row", "col"),
        P("row"),
        P("row", "col"),
        P("col"),
        P("row", "col"),
        P("row"),
        P("row", ("dp", "col")),
    )
    return jax.shard_map(
        body,
        mesh=mesh,
        in_specs=placed,
        out_specs=(
            P("row", ("dp", "col")),
            P("row", ("dp", "col")),
            P(("dp", "row"), "col"),
            P(None, "row", "col"),
            P(None, "row"),
            P("row", "col"),
            P("row", "col"),
            P("row", "col"),
            P("col"),
            P("col"),
            P("row", "col"),
            P("row"),
            P("row", "col"),
            P("col"),
            P("row", "col"),
            P("row"),
        ),
        check_vma=False,
    )
```

```python
from functools import partial

import jax
import jax.numpy as jnp
from jax import lax
from jax.sharding import PartitionSpec as P

D = 768
HEAD_DIM = 64
LEN = 256
ORDER = (0, 2, 1, 3)
F32 = jnp.float32
BF16 = jnp.bfloat16


def contract(left, right, left_dim, right_dim):
    return lax.dot_general(
        left, right, (((left_dim,), (right_dim,)), ((), ())), preferred_element_type=F32
    )


def contract_heads(left, right, left_dim, right_dim):
    return lax.dot_general(
        left, right, (((left_dim,), (right_dim,)), ((0,), (0,))), preferred_element_type=F32
    )


def swap_row(value, offset):
    size = lax.axis_size("row")
    return lax.ppermute(value, "row", [(i, i ^ offset) for i in range(size)])


def swap_col(value):
    return lax.ppermute(value, "col", [(0, 1), (1, 0)])


def after(value, earlier):
    return lax.optimization_barrier((value, earlier))[0]


def gather_row(shard, far=None):
    if far is None:
        far = swap_row(shard, 2)
    return jnp.concatenate([shard, far, swap_row(shard, 1), swap_row(far, 1)], axis=0)


def pair_sum(partial_sum):
    mine = partial_sum.astype(BF16)
    return mine.astype(F32) + swap_col(mine).astype(F32)


def near_sum(left, right):
    half = left.shape[0] // 2
    quarter = half // 2
    other = swap_row(contract(left[half:], right, 1, 1).astype(BF16), 1)
    own = contract(left[:quarter], right, 1, 1) + other[:quarter].astype(F32)
    far = contract(left[quarter:half], right, 1, 1) + other[quarter:].astype(F32)
    return own, far.astype(BF16)


def far_sum(near):
    return (near[0] + swap_row(near[1], 2).astype(F32)).astype(BF16)


def dp_pairs():
    size = lax.axis_size("dp")
    inward = [(i, i + 1) if i % 4 == 0 else (i, i - 1) for i in range(size) if i % 4 in (0, 3)]
    middle = [(i, i ^ 3) for i in range(size) if i % 4 in (1, 2)]
    return inward, middle, [(b, a) for a, b in inward]


def dp_first(value):
    return (value.astype(F32) + lax.ppermute(value, "dp", dp_pairs()[0]).astype(F32)).astype(BF16)


def dp_second(first):
    size = lax.axis_size("dp")
    total = first.astype(F32) + lax.ppermute(first, "dp", dp_pairs()[1]).astype(F32)
    total = total.astype(BF16)
    step = 4
    while step < size:
        other = lax.ppermute(total, "dp", [(i, i ^ step) for i in range(size)])
        total = (total.astype(F32) + other.astype(F32)).astype(BF16)
        step *= 2
    return total


def dp_third(total):
    place = lax.axis_index("dp") % 4
    inner = jnp.logical_or(place == 1, place == 2)
    back = lax.ppermute(total, "dp", dp_pairs()[2])
    return jnp.where(inner, total, back).astype(F32)


def gather_dp(value):
    size = lax.axis_size("dp")
    place = lax.axis_index("dp")
    step = 1
    while step < size:
        other = lax.ppermute(value, "dp", [(i, i ^ step) for i in range(size)])
        upper = (place // step) % 2 == 1
        value = jnp.concatenate(
            [jnp.where(upper, other, value), jnp.where(upper, value, other)], axis=0
        )
        step *= 2
    return value


def beside(columns):
    lane = lax.broadcasted_iota(jnp.int32, (1, len(columns)), 1)
    return sum(jnp.where(lane == i, column, 0.0) for i, column in enumerate(columns))


def latent_of(local, row, col):
    per_col = local.shape[1] // LEN
    both = jnp.concatenate([local, swap_col(local)], axis=1)

    def block(latent):
        place = jnp.where(latent // per_col == col, 0, per_col) + latent % per_col
        return lax.dynamic_slice_in_dim(both, place * LEN, LEN, axis=1)

    return jnp.concatenate(
        [block(row)] + [swap_row(block(row ^ k), k) for k in ORDER[1:]], axis=0
    )


def spread_out(full, row, col):
    rows, cols = lax.axis_size("row"), lax.axis_size("col")
    per_col = rows // cols
    width = full.shape[0] // rows
    got = {0: full[:width]}
    for place, k in enumerate(ORDER):
        if k:
            pairs = [(r * cols + r // per_col, (r ^ k) * cols + r // per_col) for r in range(rows)]
            got[k] = lax.ppermute(
                full[place * width : (place + 1) * width], ("row", "col"), pairs
            )
    here = row // per_col == col
    first = jnp.where(here, got[0], got[2])
    second = jnp.where(here, got[1], got[3])
    even = row % 2 == 0
    return jnp.concatenate(
        [jnp.where(even, first, second), jnp.where(even, second, first)], axis=1
    )


def normalize(values):
    centre = jnp.mean(values, axis=0, keepdims=True)
    moved = values - centre
    inverse = lax.rsqrt(jnp.mean(moved * moved, axis=0, keepdims=True) + 1e-06)
    return moved * inverse, inverse


def normalize_back(grad, normed, inverse):
    return inverse * (
        grad
        - jnp.mean(grad, axis=0, keepdims=True)
        - normed * jnp.mean(grad * normed, axis=0, keepdims=True)
    )


def body(
    tokens,
    condition,
    w_mod,
    b_mod,
    w_query,
    w_key,
    w_value,
    b_query,
    b_value,
    w_out,
    b_out,
    w_up,
    b_up,
    w_down,
    b_down,
    cotangent,
):
    row = lax.axis_index("row")
    col = lax.axis_index("col")
    rows = lax.axis_size("row")
    width_row = tokens.shape[0]
    width_col = w_query.shape[1]
    heads = width_col // HEAD_DIM

    condition_float = condition.astype(F32)
    silu_cond = jax.nn.silu(condition_float).astype(BF16)
    cond_rows = jnp.concatenate(
        [silu_cond] + [swap_row(silu_cond, k) for k in ORDER[1:]], axis=0
    )
    w_joined_own = jnp.concatenate([after(w_query, cond_rows), w_key, w_value], axis=1)
    far_joined = swap_row(w_joined_own, 2)
    mod_flat = w_mod.reshape(-1, w_mod.shape[2])
    terms = contract(cond_rows, mod_flat, 1, 1)
    terms = terms + swap_col(terms)
    terms = terms.reshape(rows, 6, width_row) + b_mod.astype(F32)[None]
    extra = jnp.stack([b_out, b_down]).astype(F32)
    packed = jnp.concatenate([terms, jnp.broadcast_to(extra[None], (rows, 2, width_row))], axis=1)
    vectors = jnp.concatenate(
        [packed[0]] + [swap_row(packed[i], k) for i, k in enumerate(ORDER) if k], axis=1
    )
    columns = vectors.T
    local_tokens = latent_of(tokens, row, col)
    held = (local_tokens, far_joined)
    far_out = swap_row(after(w_out, held), 2)
    far_up = swap_row(after(w_up, far_out), 2)
    far_down = swap_row(after(w_down, far_up), 2)
    cot = latent_of(after(cotangent, far_up), row, col).astype(F32)
    w_joined = gather_row(w_joined_own, far_joined)
    w_out_all = gather_row(w_out, far_out)
    w_up_all = gather_row(w_up, far_up)
    w_down_all = gather_row(w_down, far_down)
    shift_attn, scale_attn, gate_attn, shift_mlp, scale_mlp, gate_mlp, bias_out, bias_down = (
        columns[:, i : i + 1] for i in range(8)
    )

    x = local_tokens.astype(F32)
    normed_attn, inverse_attn = normalize(x)
    hidden_attn = (normed_attn * (1.0 + scale_attn) + shift_attn).astype(BF16)
    joined = contract(w_joined, hidden_attn, 0, 0)

    def split_heads(matrix):
        return matrix.reshape(heads, HEAD_DIM, LEN)

    queries = split_heads((joined[:width_col] + b_query.astype(F32)[:, None]).astype(BF16))
    keys = split_heads(joined[width_col : 2 * width_col].astype(BF16))
    values = split_heads((joined[2 * width_col :] + b_value.astype(F32)[:, None]).astype(BF16))
    scale_factor = HEAD_DIM ** (-0.5)
    scores = contract_heads(queries, keys, 1, 1) * scale_factor
    exponent = jnp.exp(scores - jnp.max(scores, axis=-1, keepdims=True))
    full_probs = exponent / jnp.sum(exponent, axis=-1, keepdims=True)
    probabilities = full_probs.astype(BF16)
    attended = contract_heads(values, probabilities, 2, 2).reshape(width_col, LEN).astype(BF16)
    projected = pair_sum(contract(w_out_all, attended, 1, 0)) + bias_out
    residual = x + gate_attn * projected

    normed_mlp, inverse_mlp = normalize(residual)
    hidden_mlp = (normed_mlp * (1.0 + scale_mlp) + shift_mlp).astype(BF16)
    upward = contract(w_up_all, hidden_mlp, 0, 0) + b_up.astype(F32)[:, None]
    activated, gelu_back = jax.vjp(partial(jax.nn.gelu, approximate=True), upward)
    activated = activated.astype(BF16)

    grad_down = (cot * gate_mlp).astype(BF16)
    grad_activated = contract(w_down_all, grad_down, 0, 0)
    grad_b_down = jnp.sum(grad_down.astype(F32), axis=1, keepdims=True)
    grad_upward = gelu_back(grad_activated)[0].astype(BF16)
    near_down = near_sum(grad_down, activated)
    grad_hidden = pair_sum(contract(w_up_all, grad_upward, 1, 0))
    near_up = near_sum(hidden_mlp, grad_upward)
    grad_b_up = jnp.sum(grad_upward.astype(F32), axis=1, keepdims=True)
    grad_hidden, near_down, near_up = lax.optimization_barrier((grad_hidden, near_down, near_up))
    sum_down = far_sum(near_down)
    grad_scale_mlp = jnp.sum(grad_hidden * normed_mlp, axis=1, keepdims=True)
    grad_shift_mlp = jnp.sum(grad_hidden, axis=1, keepdims=True)
    grad_residual = cot + normalize_back(grad_hidden * (1.0 + scale_mlp), normed_mlp, inverse_mlp)

    down_partial = after(contract(w_down_all, activated, 1, 0), grad_hidden)
    downward = pair_sum(down_partial) + bias_down
    output = spread_out((residual + gate_mlp * downward).astype(BF16), row, col)
    grad_gate_mlp = jnp.sum(cot * downward, axis=1, keepdims=True)

    grad_gate_attn = jnp.sum(grad_residual * projected, axis=1, keepdims=True)
    grad_projected = (grad_residual * gate_attn).astype(BF16)
    near_out = near_sum(grad_projected, attended)
    grad_b_out = jnp.sum(grad_projected.astype(F32), axis=1, keepdims=True)
    grad_heads = split_heads(contract(w_out_all, grad_projected, 0, 0).astype(BF16))
    grad_probs = contract_heads(grad_heads, values, 1, 1)
    grad_values = contract_heads(grad_heads, probabilities, 2, 1)
    grad_probs, sum_down = lax.optimization_barrier((grad_probs, sum_down))
    total_down = lax.psum(sum_down, "dp")
    grad_w_down = total_down.astype(F32)
    sum_up = far_sum(near_up)
    inner = jnp.sum(full_probs * grad_probs, axis=-1, keepdims=True)
    grad_scores = (full_probs * (grad_probs - inner)).astype(BF16)
    grad_queries = contract_heads(keys, grad_scores, 2, 2) * scale_factor
    grad_keys = contract_heads(queries, grad_scores, 2, 1) * scale_factor
    grad_joined = jnp.concatenate(
        [part.reshape(width_col, LEN).astype(BF16) for part in (grad_queries, grad_keys, grad_values)],
        axis=0,
    )
    sum_out = far_sum(near_out)
    grad_joined, sum_up, sum_out = lax.optimization_barrier((grad_joined, sum_up, sum_out))
    grad_w_up, grad_w_out = (t.astype(F32) for t in lax.psum((after(sum_up, total_down), sum_out), "dp"))
    grad_hidden = pair_sum(contract(w_joined, grad_joined, 1, 0))
    near_joined = near_sum(hidden_attn, grad_joined)
    grad_b_joined = jnp.sum(grad_joined.astype(F32), axis=1, keepdims=True)
    sum_joined = far_sum(near_joined)
    grad_scale_attn = jnp.sum(grad_hidden * normed_attn, axis=1, keepdims=True)
    grad_shift_attn = jnp.sum(grad_hidden, axis=1, keepdims=True)
    grad_x = grad_residual + normalize_back(
        grad_hidden * (1.0 + scale_attn), normed_attn, inverse_attn
    )
    grad_tokens = spread_out(grad_x.astype(BF16), row, col)

    own_vectors = beside(
        [
            grad_shift_attn,
            grad_scale_attn,
            grad_gate_attn,
            grad_shift_mlp,
            grad_scale_mlp,
            grad_gate_mlp,
            grad_b_down,
            grad_b_out,
        ]
    ).astype(BF16).T
    bias_grads = jnp.concatenate(
        [grad_b_up, grad_b_joined[:width_col], grad_b_joined[2 * width_col :]]
    ).reshape(-1, width_row).astype(BF16)
    pieces = [
        jnp.concatenate([own_vectors[:, i * width_row : (i + 1) * width_row], bias_grads])
        for i in range(rows)
    ]
    by_latent = jnp.stack([pieces[0]] + [swap_row(pieces[i], k) for i, k in enumerate(ORDER) if k])
    grad_mod = by_latent[:, :6].reshape(rows, -1)
    grad_silu = contract(grad_mod, mod_flat, 1, 0)
    grad_silu = grad_silu[0:1] + sum(
        swap_row(grad_silu[i : i + 1], k) for i, k in enumerate(ORDER) if k
    )
    grad_condition = jax.vjp(jax.nn.silu, condition_float)[1](grad_silu)[0]
    bias_terms = by_latent[:, 8:].astype(F32)
    bias_terms = (bias_terms[0] + bias_terms[1]) + (bias_terms[2] + bias_terms[3])
    message = jnp.concatenate(
        [
            by_latent[:, :8].reshape(rows, -1),
            cond_rows,
            bias_terms.astype(BF16).reshape(rows, -1),
        ],
        axis=1,
    )
    everyone = gather_dp(message)
    all_mod = everyone[:, : 6 * width_row]
    all_cond = everyone[:, 8 * width_row : 8 * width_row + width_col]
    grad_w_mod = contract(all_mod, all_cond, 0, 0).reshape(w_mod.shape)
    sums = jnp.sum(everyone[:, : 8 * width_row].astype(F32), axis=0)
    grad_b_mod = sums[: 6 * width_row].reshape(b_mod.shape)
    grad_b_down = sums[6 * width_row : 7 * width_row]
    grad_b_out = sums[7 * width_row :]
    bias_parts = everyone[:, 8 * width_row + width_col :].astype(F32)
    bias_sums = jnp.sum(bias_parts.reshape(-1, rows, bias_parts.shape[1]), axis=0).reshape(-1)
    hidden_width = grad_b_up.shape[0]

    grad_w_joined = dp_third(dp_second(dp_first(sum_joined)))
    return (
        output,
        grad_tokens.astype(F32),
        grad_condition,
        grad_w_mod,
        grad_b_mod,
        grad_w_joined[:, :width_col],
        grad_w_joined[:, width_col : 2 * width_col],
        grad_w_joined[:, 2 * width_col :],
        bias_sums[hidden_width : hidden_width + width_col],
        bias_sums[hidden_width + width_col :],
        grad_w_out,
        grad_b_out,
        grad_w_up,
        bias_sums[:hidden_width],
        grad_w_down,
        grad_b_down,
    )


def solution(mesh):
    placed = (
        P("row", ("dp", "col")),
        P(("dp", "row"), "col"),
        P(None, "row", "col"),
        P(None, "row"),
        P("row", "col"),
        P("row", "col"),
        P("row", "col"),
        P("col"),
        P("col"),
        P("row", "col"),
        P("row"),
        P("row", "col"),
        P("col"),
        P("row", "col"),
        P("row"),
        P("row", ("dp", "col")),
    )
    return jax.shard_map(
        body,
        mesh=mesh,
        in_specs=placed,
        out_specs=(
            P("row", ("dp", "col")),
            P("row", ("dp", "col")),
            P(("dp", "row"), "col"),
            P(None, "row", "col"),
            P(None, "row"),
            P("row", "col"),
            P("row", "col"),
            P("row", "col"),
            P("col"),
            P("col"),
            P("row", "col"),
            P("row"),
            P("row", "col"),
            P("col"),
            P("row", "col"),
            P("row"),
        ),
        check_vma=False,
    )
```

```python
from functools import partial

import jax
import jax.numpy as jnp
from jax import lax
from jax.sharding import PartitionSpec as P

D = 768
HEAD_DIM = 64
LEN = 256
ORDER = (0, 2, 1, 3)
F32 = jnp.float32
BF16 = jnp.bfloat16


def contract(left, right, left_dim, right_dim):
    return lax.dot_general(
        left, right, (((left_dim,), (right_dim,)), ((), ())), preferred_element_type=F32
    )


def contract_heads(left, right, left_dim, right_dim):
    return lax.dot_general(
        left, right, (((left_dim,), (right_dim,)), ((0,), (0,))), preferred_element_type=F32
    )


def swap_row(value, offset):
    size = lax.axis_size("row")
    return lax.ppermute(value, "row", [(i, i ^ offset) for i in range(size)])


def swap_col(value):
    return lax.ppermute(value, "col", [(0, 1), (1, 0)])


def after(value, earlier):
    return lax.optimization_barrier((value, earlier))[0]


def gather_row(shard, far=None):
    if far is None:
        far = swap_row(shard, 2)
    return jnp.concatenate([shard, far, swap_row(shard, 1), swap_row(far, 1)], axis=0)


def pair_sum(partial_sum):
    mine = partial_sum.astype(BF16)
    return mine.astype(F32) + swap_col(mine).astype(F32)


def near_sum(left, right):
    half = left.shape[0] // 2
    quarter = half // 2
    other = swap_row(contract(left[half:], right, 1, 1).astype(BF16), 1)
    own = contract(left[:quarter], right, 1, 1) + other[:quarter].astype(F32)
    far = contract(left[quarter:half], right, 1, 1) + other[quarter:].astype(F32)
    return own, far.astype(BF16)


def far_sum(near):
    return (near[0] + swap_row(near[1], 2).astype(F32)).astype(BF16)


def dp_pairs():
    size = lax.axis_size("dp")
    inward = [(i, i + 1) if i % 4 == 0 else (i, i - 1) for i in range(size) if i % 4 in (0, 3)]
    middle = [(i, i ^ 3) for i in range(size) if i % 4 in (1, 2)]
    return inward, middle, [(b, a) for a, b in inward]


def dp_first(value):
    return (value.astype(F32) + lax.ppermute(value, "dp", dp_pairs()[0]).astype(F32)).astype(BF16)


def dp_second(first):
    size = lax.axis_size("dp")
    total = first.astype(F32) + lax.ppermute(first, "dp", dp_pairs()[1]).astype(F32)
    total = total.astype(BF16)
    step = 4
    while step < size:
        other = lax.ppermute(total, "dp", [(i, i ^ step) for i in range(size)])
        total = (total.astype(F32) + other.astype(F32)).astype(BF16)
        step *= 2
    return total


def dp_third(total):
    place = lax.axis_index("dp") % 4
    inner = jnp.logical_or(place == 1, place == 2)
    back = lax.ppermute(total, "dp", dp_pairs()[2])
    return jnp.where(inner, total, back).astype(F32)


def gather_dp(value):
    size = lax.axis_size("dp")
    place = lax.axis_index("dp")
    step = 1
    while step < size:
        other = lax.ppermute(value, "dp", [(i, i ^ step) for i in range(size)])
        upper = (place // step) % 2 == 1
        value = jnp.concatenate(
            [jnp.where(upper, other, value), jnp.where(upper, value, other)], axis=0
        )
        step *= 2
    return value


def beside(columns):
    lane = lax.broadcasted_iota(jnp.int32, (1, len(columns)), 1)
    return sum(jnp.where(lane == i, column, 0.0) for i, column in enumerate(columns))


def both_cols(local):
    return jnp.concatenate([local, swap_col(local)], axis=1)


def latent_of(both, row, col):
    per_col = both.shape[1] // LEN // lax.axis_size("col")

    def block(latent):
        place = jnp.where(latent // per_col == col, 0, per_col) + latent % per_col
        return lax.dynamic_slice_in_dim(both, place * LEN, LEN, axis=1)

    return jnp.concatenate(
        [block(row)] + [swap_row(block(row ^ k), k) for k in ORDER[1:]], axis=0
    )


def spread_out(full, row, col):
    rows, cols = lax.axis_size("row"), lax.axis_size("col")
    per_col = rows // cols
    width = full.shape[0] // rows
    got = {0: full[:width]}
    for place, k in enumerate(ORDER):
        if k:
            pairs = [(r * cols + r // per_col, (r ^ k) * cols + r // per_col) for r in range(rows)]
            got[k] = lax.ppermute(
                full[place * width : (place + 1) * width], ("row", "col"), pairs
            )
    here = row // per_col == col
    first = jnp.where(here, got[0], got[2])
    second = jnp.where(here, got[1], got[3])
    even = row % 2 == 0
    return jnp.where(even, first, second), jnp.where(even, second, first)


def normalize(values):
    centre = jnp.mean(values, axis=0, keepdims=True)
    moved = values - centre
    inverse = lax.rsqrt(jnp.mean(moved * moved, axis=0, keepdims=True) + 1e-06)
    return moved * inverse, inverse


def normalize_back(grad, normed, inverse):
    return inverse * (
        grad
        - jnp.mean(grad, axis=0, keepdims=True)
        - normed * jnp.mean(grad * normed, axis=0, keepdims=True)
    )


def body(
    tokens,
    condition,
    w_mod,
    b_mod,
    w_query,
    w_key,
    w_value,
    b_query,
    b_value,
    w_out,
    b_out,
    w_up,
    b_up,
    w_down,
    b_down,
    cotangent,
):
    row = lax.axis_index("row")
    col = lax.axis_index("col")
    rows = lax.axis_size("row")
    width_row = tokens.shape[0]
    width_col = w_query.shape[1]
    heads = width_col // HEAD_DIM

    condition_float = condition.astype(F32)
    silu_cond = jax.nn.silu(condition_float).astype(BF16)
    cond_rows = jnp.concatenate(
        [silu_cond] + [swap_row(silu_cond, k) for k in ORDER[1:]], axis=0
    )
    w_joined_own = jnp.concatenate([after(w_query, cond_rows), w_key, w_value], axis=1)
    far_joined = swap_row(w_joined_own, 2)
    mod_flat = w_mod.reshape(-1, w_mod.shape[2])
    terms = contract(cond_rows, mod_flat, 1, 1)
    terms = terms + swap_col(terms)
    terms, far_joined, both_tokens, both_cot = lax.optimization_barrier(
        (terms, far_joined, both_cols(tokens), both_cols(cotangent))
    )
    terms = terms.reshape(rows, 6, width_row) + b_mod.astype(F32)[None]
    extra = jnp.stack([b_out, b_down]).astype(F32)
    packed = jnp.concatenate([terms, jnp.broadcast_to(extra[None], (rows, 2, width_row))], axis=1)
    vectors = jnp.concatenate(
        [packed[0]] + [swap_row(packed[i], k) for i, k in enumerate(ORDER) if k], axis=1
    )
    columns = vectors.T
    local_tokens = latent_of(both_tokens, row, col)
    far_out = swap_row(after(w_out, far_joined), 2)
    far_up = swap_row(after(w_up, far_joined), 2)
    w_joined = gather_row(w_joined_own, far_joined)
    shift_attn, scale_attn, gate_attn, shift_mlp, scale_mlp, gate_mlp, bias_out, bias_down = (
        columns[:, i : i + 1] for i in range(8)
    )

    x = local_tokens.astype(F32)
    normed_attn, inverse_attn = normalize(x)
    hidden_attn = (normed_attn * (1.0 + scale_attn) + shift_attn).astype(BF16)
    joined = contract(w_joined, hidden_attn, 0, 0)

    def split_heads(matrix):
        return matrix.reshape(heads, HEAD_DIM, LEN)

    queries = split_heads((joined[:width_col] + b_query.astype(F32)[:, None]).astype(BF16))
    keys = split_heads(joined[width_col : 2 * width_col].astype(BF16))
    values = split_heads((joined[2 * width_col :] + b_value.astype(F32)[:, None]).astype(BF16))
    scale_factor = HEAD_DIM ** (-0.5)
    scores = contract_heads(queries, keys, 1, 1) * scale_factor
    exponent = jnp.exp(scores - jnp.max(scores, axis=-1, keepdims=True))
    full_probs = exponent / jnp.sum(exponent, axis=-1, keepdims=True)
    probabilities = full_probs.astype(BF16)
    attended = contract_heads(values, probabilities, 2, 2).reshape(width_col, LEN).astype(BF16)
    attended, far_out, far_up = lax.optimization_barrier((attended, far_out, far_up))
    w_out_all = gather_row(w_out, far_out)
    w_up_all = gather_row(w_up, far_up)
    far_down = swap_row(after(w_down, far_up), 2)
    cot = latent_of(after(both_cot, far_up), row, col).astype(F32)
    projected = pair_sum(contract(w_out_all, attended, 1, 0)) + bias_out
    projected, far_down, cot = lax.optimization_barrier((projected, far_down, cot))
    w_down_all = gather_row(w_down, far_down)
    residual = x + gate_attn * projected

    normed_mlp, inverse_mlp = normalize(residual)
    hidden_mlp = (normed_mlp * (1.0 + scale_mlp) + shift_mlp).astype(BF16)
    upward = contract(w_up_all, hidden_mlp, 0, 0) + b_up.astype(F32)[:, None]
    activated, gelu_back = jax.vjp(partial(jax.nn.gelu, approximate=True), upward)
    activated = activated.astype(BF16)

    grad_down = (cot * gate_mlp).astype(BF16)
    grad_activated = contract(w_down_all, grad_down, 0, 0)
    grad_b_down = jnp.sum(grad_down.astype(F32), axis=1, keepdims=True)
    grad_upward = gelu_back(grad_activated)[0].astype(BF16)
    near_down = near_sum(grad_down, activated)
    grad_hidden = pair_sum(contract(w_up_all, grad_upward, 1, 0))
    near_up = near_sum(hidden_mlp, grad_upward)
    grad_b_up = jnp.sum(grad_upward.astype(F32), axis=1, keepdims=True)
    grad_hidden, near_down, near_up = lax.optimization_barrier((grad_hidden, near_down, near_up))
    sum_down = far_sum(near_down)
    grad_scale_mlp = jnp.sum(grad_hidden * normed_mlp, axis=1, keepdims=True)
    grad_shift_mlp = jnp.sum(grad_hidden, axis=1, keepdims=True)
    grad_residual = cot + normalize_back(grad_hidden * (1.0 + scale_mlp), normed_mlp, inverse_mlp)

    down_partial = after(contract(w_down_all, activated, 1, 0), grad_hidden)
    downward = pair_sum(down_partial) + bias_down
    output = (residual + gate_mlp * downward).astype(BF16)
    grad_gate_mlp = jnp.sum(cot * downward, axis=1, keepdims=True)

    grad_gate_attn = jnp.sum(grad_residual * projected, axis=1, keepdims=True)
    grad_projected = (grad_residual * gate_attn).astype(BF16)
    near_out = near_sum(grad_projected, attended)
    grad_b_out = jnp.sum(grad_projected.astype(F32), axis=1, keepdims=True)
    grad_heads = split_heads(contract(w_out_all, grad_projected, 0, 0).astype(BF16))
    grad_probs = contract_heads(grad_heads, values, 1, 1)
    grad_values = contract_heads(grad_heads, probabilities, 2, 1)
    grad_probs, sum_down = lax.optimization_barrier((grad_probs, sum_down))
    first_down = dp_first(sum_down)
    sum_up = far_sum(near_up)
    inner = jnp.sum(full_probs * grad_probs, axis=-1, keepdims=True)
    grad_scores = (full_probs * (grad_probs - inner)).astype(BF16)
    grad_scores, first_down, sum_up = lax.optimization_barrier((grad_scores, first_down, sum_up))
    total_down = dp_second(first_down)
    first_up = dp_first(sum_up)
    grad_queries = contract_heads(keys, grad_scores, 2, 2) * scale_factor
    grad_keys = contract_heads(queries, grad_scores, 2, 1) * scale_factor
    grad_joined = jnp.concatenate(
        [part.reshape(width_col, LEN).astype(BF16) for part in (grad_queries, grad_keys, grad_values)],
        axis=0,
    )
    sum_out = far_sum(near_out)
    grad_hidden = pair_sum(contract(w_joined, grad_joined, 1, 0))
    near_joined = near_sum(hidden_attn, grad_joined)
    grad_b_joined = jnp.sum(grad_joined.astype(F32), axis=1, keepdims=True)
    grad_hidden, total_down, first_up, sum_out = lax.optimization_barrier(
        (grad_hidden, total_down, first_up, sum_out)
    )
    sum_joined = far_sum(near_joined)
    grad_w_down = dp_third(total_down)
    total_up = dp_second(first_up)
    first_out = dp_first(sum_out)
    grad_scale_attn = jnp.sum(grad_hidden * normed_attn, axis=1, keepdims=True)
    grad_shift_attn = jnp.sum(grad_hidden, axis=1, keepdims=True)
    grad_x = grad_residual + normalize_back(
        grad_hidden * (1.0 + scale_attn), normed_attn, inverse_attn
    )
    spread = spread_out(jnp.concatenate([output, grad_x.astype(BF16)], axis=1), row, col)
    output = jnp.concatenate([part[:, :LEN] for part in spread], axis=1)
    grad_tokens = jnp.concatenate([part[:, LEN:] for part in spread], axis=1)

    own_vectors = beside(
        [
            grad_shift_attn,
            grad_scale_attn,
            grad_gate_attn,
            grad_shift_mlp,
            grad_scale_mlp,
            grad_gate_mlp,
            grad_b_down,
            grad_b_out,
        ]
    ).astype(BF16).T
    bias_grads = jnp.concatenate(
        [grad_b_up, grad_b_joined[:width_col], grad_b_joined[2 * width_col :]]
    ).reshape(-1, width_row).astype(BF16)
    pieces = [
        jnp.concatenate([own_vectors[:, i * width_row : (i + 1) * width_row], bias_grads])
        for i in range(rows)
    ]
    by_latent = jnp.stack([pieces[0]] + [swap_row(pieces[i], k) for i, k in enumerate(ORDER) if k])
    grad_mod = by_latent[:, :6].reshape(rows, -1)
    grad_silu = contract(grad_mod, mod_flat, 1, 0)
    grad_silu = grad_silu[0:1] + sum(
        swap_row(grad_silu[i : i + 1], k) for i, k in enumerate(ORDER) if k
    )
    grad_condition = jax.vjp(jax.nn.silu, condition_float)[1](grad_silu)[0]
    bias_terms = by_latent[:, 8:].astype(F32)
    bias_terms = (bias_terms[0] + bias_terms[1]) + (bias_terms[2] + bias_terms[3])
    message = jnp.concatenate(
        [
            by_latent[:, :8].reshape(rows, -1),
            cond_rows,
            bias_terms.astype(BF16).reshape(rows, -1),
        ],
        axis=1,
    )
    everyone = gather_dp(message)
    all_mod = everyone[:, : 6 * width_row]
    all_cond = everyone[:, 8 * width_row : 8 * width_row + width_col]
    grad_w_mod = contract(all_mod, all_cond, 0, 0).reshape(w_mod.shape)
    sums = jnp.sum(everyone[:, : 8 * width_row].astype(F32), axis=0)
    grad_b_mod = sums[: 6 * width_row].reshape(b_mod.shape)
    grad_b_down = sums[6 * width_row : 7 * width_row]
    grad_b_out = sums[7 * width_row :]
    bias_parts = everyone[:, 8 * width_row + width_col :].astype(F32)
    bias_sums = jnp.sum(bias_parts.reshape(-1, rows, bias_parts.shape[1]), axis=0).reshape(-1)
    hidden_width = grad_b_up.shape[0]

    first_joined = dp_first(sum_joined)
    total_out = dp_second(first_out)
    grad_w_up = dp_third(total_up)
    total_joined = dp_second(first_joined)
    grad_w_out = dp_third(total_out)
    grad_w_joined = dp_third(total_joined)
    return (
        output,
        grad_tokens.astype(F32),
        grad_condition,
        grad_w_mod,
        grad_b_mod,
        grad_w_joined[:, :width_col],
        grad_w_joined[:, width_col : 2 * width_col],
        grad_w_joined[:, 2 * width_col :],
        bias_sums[hidden_width : hidden_width + width_col],
        bias_sums[hidden_width + width_col :],
        grad_w_out,
        grad_b_out,
        grad_w_up,
        bias_sums[:hidden_width],
        grad_w_down,
        grad_b_down,
    )


def solution(mesh):
    placed = (
        P("row", ("dp", "col")),
        P(("dp", "row"), "col"),
        P(None, "row", "col"),
        P(None, "row"),
        P("row", "col"),
        P("row", "col"),
        P("row", "col"),
        P("col"),
        P("col"),
        P("row", "col"),
        P("row"),
        P("row", "col"),
        P("col"),
        P("row", "col"),
        P("row"),
        P("row", ("dp", "col")),
    )
    return jax.shard_map(
        body,
        mesh=mesh,
        in_specs=placed,
        out_specs=(
            P("row", ("dp", "col")),
            P("row", ("dp", "col")),
            P(("dp", "row"), "col"),
            P(None, "row", "col"),
            P(None, "row"),
            P("row", "col"),
            P("row", "col"),
            P("row", "col"),
            P("col"),
            P("col"),
            P("row", "col"),
            P("row"),
            P("row", "col"),
            P("col"),
            P("row", "col"),
            P("row"),
        ),
        check_vma=False,
    )
```

```python
from functools import partial

import jax
import jax.numpy as jnp
from jax import lax
from jax.sharding import PartitionSpec as P

D = 768
HEAD_DIM = 64
LEN = 256
ORDER = (0, 2, 1, 3)
F32 = jnp.float32
BF16 = jnp.bfloat16


def contract(left, right, left_dim, right_dim):
    return lax.dot_general(
        left, right, (((left_dim,), (right_dim,)), ((), ())), preferred_element_type=F32
    )


def contract_heads(left, right, left_dim, right_dim):
    return lax.dot_general(
        left, right, (((left_dim,), (right_dim,)), ((0,), (0,))), preferred_element_type=F32
    )


def swap_row(value, offset):
    size = lax.axis_size("row")
    return lax.ppermute(value, "row", [(i, i ^ offset) for i in range(size)])


def swap_col(value):
    return lax.ppermute(value, "col", [(0, 1), (1, 0)])


def after(value, earlier):
    return lax.optimization_barrier((value, earlier))[0]


def gather_row(shard, far=None):
    if far is None:
        far = swap_row(shard, 2)
    return jnp.concatenate([shard, far, swap_row(shard, 1), swap_row(far, 1)], axis=0)


def pair_sum(partial_sum):
    mine = partial_sum.astype(BF16)
    return mine.astype(F32) + swap_col(mine).astype(F32)


def near_sum(left, right):
    half = left.shape[0] // 2
    quarter = half // 2
    other = swap_row(contract(left[half:], right, 1, 1).astype(BF16), 1)
    own = contract(left[:quarter], right, 1, 1) + other[:quarter].astype(F32)
    far = contract(left[quarter:half], right, 1, 1) + other[quarter:].astype(F32)
    return own, far.astype(BF16)


def far_sum(near):
    return (near[0] + swap_row(near[1], 2).astype(F32)).astype(BF16)


def dp_pairs():
    size = lax.axis_size("dp")
    inward = [(i, i + 1) if i % 4 == 0 else (i, i - 1) for i in range(size) if i % 4 in (0, 3)]
    middle = [(i, i ^ 3) for i in range(size) if i % 4 in (1, 2)]
    return inward, middle, [(b, a) for a, b in inward]


def dp_first(value):
    return (value.astype(F32) + lax.ppermute(value, "dp", dp_pairs()[0]).astype(F32)).astype(BF16)


def dp_second(first):
    size = lax.axis_size("dp")
    total = first.astype(F32) + lax.ppermute(first, "dp", dp_pairs()[1]).astype(F32)
    total = total.astype(BF16)
    step = 4
    while step < size:
        other = lax.ppermute(total, "dp", [(i, i ^ step) for i in range(size)])
        total = (total.astype(F32) + other.astype(F32)).astype(BF16)
        step *= 2
    return total


def dp_third(total):
    place = lax.axis_index("dp") % 4
    inner = jnp.logical_or(place == 1, place == 2)
    back = lax.ppermute(total, "dp", dp_pairs()[2])
    return jnp.where(inner, total, back).astype(F32)


def gather_dp(value):
    size = lax.axis_size("dp")
    place = lax.axis_index("dp")
    step = 1
    while step < size:
        other = lax.ppermute(value, "dp", [(i, i ^ step) for i in range(size)])
        upper = (place // step) % 2 == 1
        value = jnp.concatenate(
            [jnp.where(upper, other, value), jnp.where(upper, value, other)], axis=0
        )
        step *= 2
    return value


def beside(columns):
    lane = lax.broadcasted_iota(jnp.int32, (1, len(columns)), 1)
    return sum(jnp.where(lane == i, column, 0.0) for i, column in enumerate(columns))


def both_cols(local):
    return jnp.concatenate([local, swap_col(local)], axis=1)


def latent_of(both, row, col):
    per_col = both.shape[1] // LEN // lax.axis_size("col")

    def block(latent):
        place = jnp.where(latent // per_col == col, 0, per_col) + latent % per_col
        return lax.dynamic_slice_in_dim(both, place * LEN, LEN, axis=1)

    return jnp.concatenate(
        [block(row)] + [swap_row(block(row ^ k), k) for k in ORDER[1:]], axis=0
    )


def spread_out(full, row, col):
    rows, cols = lax.axis_size("row"), lax.axis_size("col")
    per_col = rows // cols
    width = full.shape[0] // rows
    got = {0: full[:width]}
    for place, k in enumerate(ORDER):
        if k:
            pairs = [(r * cols + r // per_col, (r ^ k) * cols + r // per_col) for r in range(rows)]
            got[k] = lax.ppermute(
                full[place * width : (place + 1) * width], ("row", "col"), pairs
            )
    here = row // per_col == col
    first = jnp.where(here, got[0], got[2])
    second = jnp.where(here, got[1], got[3])
    even = row % 2 == 0
    return jnp.where(even, first, second), jnp.where(even, second, first)


def normalize(values):
    centre = jnp.mean(values, axis=0, keepdims=True)
    moved = values - centre
    inverse = lax.rsqrt(jnp.mean(moved * moved, axis=0, keepdims=True) + 1e-06)
    return moved * inverse, inverse


def normalize_back(grad, normed, inverse):
    return inverse * (
        grad
        - jnp.mean(grad, axis=0, keepdims=True)
        - normed * jnp.mean(grad * normed, axis=0, keepdims=True)
    )


def body(
    tokens,
    condition,
    w_mod,
    b_mod,
    w_query,
    w_key,
    w_value,
    b_query,
    b_value,
    w_out,
    b_out,
    w_up,
    b_up,
    w_down,
    b_down,
    cotangent,
):
    row = lax.axis_index("row")
    col = lax.axis_index("col")
    rows = lax.axis_size("row")
    width_row = tokens.shape[0]
    width_col = w_query.shape[1]
    heads = width_col // HEAD_DIM

    condition_float = condition.astype(F32)
    silu_cond = jax.nn.silu(condition_float).astype(BF16)
    cond_rows = jnp.concatenate(
        [silu_cond] + [swap_row(silu_cond, k) for k in ORDER[1:]], axis=0
    )
    w_joined_own = jnp.concatenate([after(w_query, cond_rows), w_key, w_value], axis=1)
    far_joined = swap_row(w_joined_own, 2)
    mod_flat = w_mod.reshape(-1, w_mod.shape[2])
    terms = contract(cond_rows, mod_flat, 1, 1)
    terms = terms + swap_col(terms)
    terms, far_joined, both_tokens, both_cot = lax.optimization_barrier(
        (terms, far_joined, both_cols(tokens), both_cols(cotangent))
    )
    terms = terms.reshape(rows, 6, width_row) + b_mod.astype(F32)[None]
    extra = jnp.stack([b_out, b_down]).astype(F32)
    packed = jnp.concatenate([terms, jnp.broadcast_to(extra[None], (rows, 2, width_row))], axis=1)
    vectors = jnp.concatenate(
        [packed[0]] + [swap_row(packed[i], k) for i, k in enumerate(ORDER) if k], axis=1
    )
    columns = vectors.T
    local_tokens = latent_of(both_tokens, row, col)
    far_out = swap_row(after(w_out, far_joined), 2)
    far_up = swap_row(after(w_up, far_joined), 2)
    local_tokens, far_out = lax.optimization_barrier((local_tokens, far_out))
    w_joined = gather_row(w_joined_own, far_joined)
    shift_attn, scale_attn, gate_attn, shift_mlp, scale_mlp, gate_mlp, bias_out, bias_down = (
        columns[:, i : i + 1] for i in range(8)
    )

    x = local_tokens.astype(F32)
    normed_attn, inverse_attn = normalize(x)
    hidden_attn = (normed_attn * (1.0 + scale_attn) + shift_attn).astype(BF16)
    hidden_attn, far_up = lax.optimization_barrier((hidden_attn, far_up))
    joined = contract(w_joined, hidden_attn, 0, 0)

    def split_heads(matrix):
        return matrix.reshape(heads, HEAD_DIM, LEN)

    queries = split_heads((joined[:width_col] + b_query.astype(F32)[:, None]).astype(BF16))
    keys = split_heads(joined[width_col : 2 * width_col].astype(BF16))
    values = split_heads((joined[2 * width_col :] + b_value.astype(F32)[:, None]).astype(BF16))
    scale_factor = HEAD_DIM ** (-0.5)
    scores = contract_heads(queries, keys, 1, 1) * scale_factor
    exponent = jnp.exp(scores - jnp.max(scores, axis=-1, keepdims=True))
    full_probs = exponent / jnp.sum(exponent, axis=-1, keepdims=True)
    probabilities = full_probs.astype(BF16)
    attended = contract_heads(values, probabilities, 2, 2).reshape(width_col, LEN).astype(BF16)
    w_out_all = gather_row(w_out, far_out)
    w_up_all = gather_row(w_up, far_up)
    far_down = swap_row(after(w_down, far_up), 2)
    cot = latent_of(after(both_cot, far_up), row, col).astype(F32)
    projected = pair_sum(contract(w_out_all, attended, 1, 0)) + bias_out
    projected, far_down, cot = lax.optimization_barrier((projected, far_down, cot))
    w_down_all = gather_row(w_down, far_down)
    residual = x + gate_attn * projected

    normed_mlp, inverse_mlp = normalize(residual)
    hidden_mlp = (normed_mlp * (1.0 + scale_mlp) + shift_mlp).astype(BF16)
    upward = contract(w_up_all, hidden_mlp, 0, 0) + b_up.astype(F32)[:, None]
    activated, gelu_back = jax.vjp(partial(jax.nn.gelu, approximate=True), upward)
    activated = activated.astype(BF16)

    grad_down = (cot * gate_mlp).astype(BF16)
    grad_activated = contract(w_down_all, grad_down, 0, 0)
    grad_b_down = jnp.sum(grad_down.astype(F32), axis=1, keepdims=True)
    grad_upward = gelu_back(grad_activated)[0].astype(BF16)
    near_down = near_sum(grad_down, activated)
    grad_hidden = pair_sum(contract(w_up_all, grad_upward, 1, 0))
    near_up = near_sum(hidden_mlp, grad_upward)
    grad_b_up = jnp.sum(grad_upward.astype(F32), axis=1, keepdims=True)
    grad_hidden, near_down, near_up = lax.optimization_barrier((grad_hidden, near_down, near_up))
    sum_down = far_sum(near_down)
    grad_scale_mlp = jnp.sum(grad_hidden * normed_mlp, axis=1, keepdims=True)
    grad_shift_mlp = jnp.sum(grad_hidden, axis=1, keepdims=True)
    grad_residual = cot + normalize_back(grad_hidden * (1.0 + scale_mlp), normed_mlp, inverse_mlp)

    down_partial = after(contract(w_down_all, activated, 1, 0), grad_hidden)
    downward = pair_sum(down_partial) + bias_down
    output = (residual + gate_mlp * downward).astype(BF16)
    grad_gate_mlp = jnp.sum(cot * downward, axis=1, keepdims=True)

    grad_gate_attn = jnp.sum(grad_residual * projected, axis=1, keepdims=True)
    grad_projected = (grad_residual * gate_attn).astype(BF16)
    near_out = near_sum(grad_projected, attended)
    grad_b_out = jnp.sum(grad_projected.astype(F32), axis=1, keepdims=True)
    grad_heads = split_heads(contract(w_out_all, grad_projected, 0, 0).astype(BF16))
    grad_probs = contract_heads(grad_heads, values, 1, 1)
    grad_values = contract_heads(grad_heads, probabilities, 2, 1)
    grad_probs, sum_down = lax.optimization_barrier((grad_probs, sum_down))
    first_down = dp_first(sum_down)
    sum_up = far_sum(near_up)
    inner = jnp.sum(full_probs * grad_probs, axis=-1, keepdims=True)
    grad_scores = (full_probs * (grad_probs - inner)).astype(BF16)
    grad_scores, first_down, sum_up = lax.optimization_barrier((grad_scores, first_down, sum_up))
    total_down = dp_second(first_down)
    first_up = dp_first(sum_up)
    grad_queries = contract_heads(keys, grad_scores, 2, 2) * scale_factor
    grad_keys = contract_heads(queries, grad_scores, 2, 1) * scale_factor
    grad_joined = jnp.concatenate(
        [part.reshape(width_col, LEN).astype(BF16) for part in (grad_queries, grad_keys, grad_values)],
        axis=0,
    )
    sum_out = far_sum(near_out)
    grad_hidden = pair_sum(contract(w_joined, grad_joined, 1, 0))
    near_joined = near_sum(hidden_attn, grad_joined)
    grad_b_joined = jnp.sum(grad_joined.astype(F32), axis=1, keepdims=True)
    grad_hidden, total_down, first_up, sum_out, near_joined = lax.optimization_barrier(
        (grad_hidden, total_down, first_up, sum_out, near_joined)
    )
    sum_joined = far_sum(near_joined)
    grad_w_down = dp_third(total_down)
    total_up = dp_second(first_up)
    first_out = dp_first(sum_out)
    grad_scale_attn = jnp.sum(grad_hidden * normed_attn, axis=1, keepdims=True)
    grad_shift_attn = jnp.sum(grad_hidden, axis=1, keepdims=True)
    grad_x = grad_residual + normalize_back(
        grad_hidden * (1.0 + scale_attn), normed_attn, inverse_attn
    )
    both_out = jnp.concatenate([output, grad_x.astype(BF16)], axis=1)
    both_out, sum_joined = lax.optimization_barrier((both_out, sum_joined))
    first_joined = dp_first(sum_joined)
    spread = spread_out(both_out, row, col)
    output = jnp.concatenate([part[:, :LEN] for part in spread], axis=1)
    grad_tokens = jnp.concatenate([part[:, LEN:] for part in spread], axis=1)

    own_vectors = beside(
        [
            grad_shift_attn,
            grad_scale_attn,
            grad_gate_attn,
            grad_shift_mlp,
            grad_scale_mlp,
            grad_gate_mlp,
            grad_b_down,
            grad_b_out,
        ]
    ).astype(BF16).T
    bias_grads = jnp.concatenate(
        [grad_b_up, grad_b_joined[:width_col], grad_b_joined[2 * width_col :]]
    ).reshape(-1, width_row).astype(BF16)
    pieces = [
        jnp.concatenate([own_vectors[:, i * width_row : (i + 1) * width_row], bias_grads])
        for i in range(rows)
    ]
    by_latent = jnp.stack([pieces[0]] + [swap_row(pieces[i], k) for i, k in enumerate(ORDER) if k])
    grad_mod = by_latent[:, :6].reshape(rows, -1)
    grad_silu = contract(grad_mod, mod_flat, 1, 0)
    grad_silu = grad_silu[0:1] + sum(
        swap_row(grad_silu[i : i + 1], k) for i, k in enumerate(ORDER) if k
    )
    grad_condition = jax.vjp(jax.nn.silu, condition_float)[1](grad_silu)[0]
    bias_terms = by_latent[:, 8:].astype(F32)
    bias_terms = (bias_terms[0] + bias_terms[1]) + (bias_terms[2] + bias_terms[3])
    message = jnp.concatenate(
        [
            by_latent[:, :8].reshape(rows, -1),
            cond_rows,
            bias_terms.astype(BF16).reshape(rows, -1),
        ],
        axis=1,
    )
    everyone, first_joined, total_up = lax.optimization_barrier(
        (gather_dp(message), first_joined, total_up)
    )
    all_mod = everyone[:, : 6 * width_row]
    all_cond = everyone[:, 8 * width_row : 8 * width_row + width_col]
    grad_w_mod = contract(all_mod, all_cond, 0, 0).reshape(w_mod.shape)
    sums = jnp.sum(everyone[:, : 8 * width_row].astype(F32), axis=0)
    grad_b_mod = sums[: 6 * width_row].reshape(b_mod.shape)
    grad_b_down = sums[6 * width_row : 7 * width_row]
    grad_b_out = sums[7 * width_row :]
    bias_parts = everyone[:, 8 * width_row + width_col :].astype(F32)
    bias_sums = jnp.sum(bias_parts.reshape(-1, rows, bias_parts.shape[1]), axis=0).reshape(-1)
    hidden_width = grad_b_up.shape[0]

    total_out = dp_second(first_out)
    grad_w_up = dp_third(total_up)
    total_joined = dp_second(first_joined)
    grad_w_out = dp_third(total_out)
    grad_w_joined = dp_third(total_joined)
    return (
        output,
        grad_tokens.astype(F32),
        grad_condition,
        grad_w_mod,
        grad_b_mod,
        grad_w_joined[:, :width_col],
        grad_w_joined[:, width_col : 2 * width_col],
        grad_w_joined[:, 2 * width_col :],
        bias_sums[hidden_width : hidden_width + width_col],
        bias_sums[hidden_width + width_col :],
        grad_w_out,
        grad_b_out,
        grad_w_up,
        bias_sums[:hidden_width],
        grad_w_down,
        grad_b_down,
    )


def solution(mesh):
    placed = (
        P("row", ("dp", "col")),
        P(("dp", "row"), "col"),
        P(None, "row", "col"),
        P(None, "row"),
        P("row", "col"),
        P("row", "col"),
        P("row", "col"),
        P("col"),
        P("col"),
        P("row", "col"),
        P("row"),
        P("row", "col"),
        P("col"),
        P("row", "col"),
        P("row"),
        P("row", ("dp", "col")),
    )
    return jax.shard_map(
        body,
        mesh=mesh,
        in_specs=placed,
        out_specs=(
            P("row", ("dp", "col")),
            P("row", ("dp", "col")),
            P(("dp", "row"), "col"),
            P(None, "row", "col"),
            P(None, "row"),
            P("row", "col"),
            P("row", "col"),
            P("row", "col"),
            P("col"),
            P("col"),
            P("row", "col"),
            P("row"),
            P("row", "col"),
            P("col"),
            P("row", "col"),
            P("row"),
        ),
        check_vma=False,
    )
```
